32 devices in a mesh: side: 2 (over core), grp: 4 (over y, x), ex: 4 (over z).
Axes of the slice: x: 2, y: 2, z: 4, core: 2. Of those that a mesh axis runs over, the one named last changes fastest.
Arguments:
- tokens: bfloat16 [48, 7168], P(('grp', 'ex'), 'side'), may hold values from -6 to 6
- expert_ids: int32 [48, 8], P(('grp', 'ex')), may hold values from 0 to 15, all different within a row; in each aligned block of 3 rows (0 to 2, 3 to 5, ...) at most 3 rows name the same one
- scores: float32 [48, 8], P(('grp', 'ex')), may hold values from -8 to 8
- gate_weight: bfloat16 [16, 7168, 2048], P('ex', 'side', 'grp'), may hold values from -0.0625 to 0.0625
- up_weight: bfloat16 [16, 7168, 2048], P('ex', 'side', 'grp'), may hold values from -0.0625 to 0.0625
- down_weight: bfloat16 [16, 2048, 7168], P('ex', None, ('side', 'grp')), may hold values from -0.125 to 0.125
Outputs:
- combined: bfloat16 [48, 7168], P(('grp', 'ex'), 'side')
The draws below stay inside these ranges and needn't reach their ends.
Inputs may be any that keep to these rules, and one draw needn't show every extreme that they name: `expert_ids`: each row names 8 different experts; every expert is named by some row.
All inputs are finite; a program needn't handle non-finite values.
Results may differ from the reference program's by a relative error of at most 0.011.
Values may be sent and summed in bfloat16 or wider, within the bound.
A program may use at most 192 MiB of HBM per device.

```python
import math
import jax
import jax.numpy as jnp
import numpy as np
from jax import lax

D = 7168
H = 2048
TOP = 8
EXPERTS = 16
TOK_DEV = 3
TOKENS = 48


def shard_levels(own_key, extent, split, smallest, largest):
    gain, own = 1.0, jax.random.fold_in(own_key, 6)
    for dim, parts in split:
        draws = jnp.exp(jax.random.uniform(jax.random.fold_in(own, dim), (parts,), jnp.float32, smallest / len(split), largest / len(split)))
        gain = gain * jnp.repeat(draws, extent[dim] // parts).reshape([-1 if axis == dim else 1 for axis in range(len(extent))])
    return gain


def assign_block(stream_key, own, number, rows, amount, top, bound, skew):
    ranking = jax.random.permutation(stream_key, amount)
    heavy_load, usual = portions_of(amount, rows * top, bound, skew, True), portions_of(amount, rows * top, bound, skew, False)
    places = jnp.arange(amount)

    def named(lengths, turn):
        used = int((lengths > 0).sum())
        fixed = max(1, used // 4)
        moved = fixed + (places - fixed + turn * (used - fixed)) % max(1, amount - fixed)
        return jnp.zeros((amount,), jnp.int32).at[ranking[jnp.where(places < fixed, places, moved)]].set(jnp.asarray(lengths, jnp.int32))

    lengths = jnp.where(number % 4 == 0, named(heavy_load, number // 4), named(usual, number - number // 4 - 1))
    mixed = jax.random.permutation(jax.random.fold_in(own, 3), amount)
    giver, taker = mixed[0:amount // 2 * 2:2], mixed[1:amount // 2 * 2:2]
    room = jnp.minimum(lengths[giver] - 1, bound - lengths[taker]) // 2
    room = jnp.where((giver == ranking[0]) | (taker == ranking[0]) | (lengths[taker] == 0), 0, jnp.maximum(room, 0))
    moved = jax.random.randint(jax.random.fold_in(own, 4), (amount // 2,), 0, 1 << 20) % (room + 1)
    lengths = lengths.at[giver].add(-moved).at[taker].add(moved)
    items = jnp.searchsorted(jnp.cumsum(lengths), jnp.arange(rows * top), side="right").astype(jnp.int32)
    table = items.reshape(top, rows).T
    table = table[jax.random.permutation(jax.random.fold_in(own, 1), rows)]
    turn = jax.random.randint(jax.random.fold_in(own, 2), (rows, 1), 0, top)
    return jnp.take_along_axis(table, (jnp.arange(top)[None, :] + turn) % top, axis=1)


def portions_of(amount, total, bound, slope, full):
    loads = [(1 << 20) // math.isqrt(grade ** slope) + 1 for grade in range(1, amount + 1)]
    largest = bound if full else min(bound, max(-(-total // amount), total * loads[0] // sum(loads)))
    least = 1 if total - largest >= amount - 1 else 0
    given, rest = [largest] + [least] * (amount - 1), total - largest - least * (amount - 1)
    while rest > 0:
        movable = [i for i in range(1, amount) if given[i] < largest] or [i for i in range(1, amount) if given[i] < bound]
        whole, left = sum([loads[i] for i in movable]), rest
        for i in movable:
            addition = min(bound - given[i], max(1, left * loads[i] // whole), rest)
            given[i] = given[i] + addition
            rest = rest - addition
    return np.array(given)


def centred(stream_key, extent, scale, reach, split=(), dtype=jnp.bfloat16):
    array = scale * jax.random.normal(stream_key, extent, jnp.float32)
    if split:
        array = array * shard_levels(stream_key, extent, split, -0.22, 0.18)
    return jnp.clip(array, -reach, reach).astype(dtype)


def setup_inputs(seed: int = 0) -> dict:
    key_list = jax.random.split(jax.random.key(seed), 7)
    tokens = centred(key_list[0], (TOKENS, D), 1.0, 6.0, ((0, 16), (1, 2)))
    expert_ids_keys = jax.random.split(jax.random.fold_in(key_list[1], 1), TOKENS // TOK_DEV)
    expert_ids_turns = jax.random.permutation(jax.random.fold_in(key_list[1], 3), TOKENS // TOK_DEV)
    expert_ids = jax.vmap(lambda own, number: assign_block(jax.random.fold_in(key_list[1], 2), own, number, TOK_DEV, EXPERTS, TOP, TOK_DEV, 2))(expert_ids_keys, expert_ids_turns).reshape((TOKENS, TOP))
    scores = centred(key_list[2], (TOKENS, TOP), 2.0, 8.0, ((0, 16),), jnp.float32)
    gate_weight = centred(key_list[3], (EXPERTS, D, H), D ** -0.5, 0.0625, ((0, 4), (1, 2), (2, 4)))
    up_weight = centred(key_list[4], (EXPERTS, D, H), D ** -0.5, 0.0625, ((0, 4), (1, 2), (2, 4)))
    down_weight = centred(key_list[5], (EXPERTS, H, D), H ** -0.5, 0.125, ((0, 4), (2, 8)))
    return {"tokens": tokens, "expert_ids": expert_ids, "scores": scores, "gate_weight": gate_weight, "up_weight": up_weight, "down_weight": down_weight}


def reference(tokens, expert_ids, scores, gate_weight, up_weight, down_weight):
    lifted = jax.nn.sigmoid(scores)
    route_weight = 2.5 * lifted / jnp.sum(lifted, axis=-1, keepdims=True)

    def add_expert(expert, total):
        gate_cols = lax.dynamic_index_in_dim(gate_weight, expert, 0, keepdims=False)
        up_cols = lax.dynamic_index_in_dim(up_weight, expert, 0, keepdims=False)
        down_rows = lax.dynamic_index_in_dim(down_weight, expert, 0, keepdims=False)
        gate = jnp.dot(tokens, gate_cols, preferred_element_type=jnp.float32)
        up_part = jnp.dot(tokens, up_cols, preferred_element_type=jnp.float32)
        hidden = (jax.nn.silu(gate) * up_part).astype(jnp.bfloat16)
        output = jnp.dot(hidden, down_rows, preferred_element_type=jnp.float32).astype(jnp.bfloat16)
        factor = jnp.sum(jnp.where(expert_ids == expert, route_weight, 0.0), axis=-1)
        return total + factor[:, None] * output.astype(jnp.float32)

    total = lax.fori_loop(0, EXPERTS, add_expert, jnp.zeros(tokens.shape, jnp.float32))
    return total.astype(jnp.bfloat16)
```

```python
import functools

import jax
import jax.numpy as jnp
from jax import lax
from jax.experimental import pallas as pl
from jax.experimental.pallas import tpu as pltpu
from jax.sharding import PartitionSpec as P

TOK = 3
ROWS = 16
PACK = ROWS // TOK


def make_fold(table, piece):
    return jnp.einsum("sech,ehd->secd", piece, table, preferred_element_type=jnp.float32)


def per_device(tokens, expert_ids, scores, gate_weight, up_weight, down_weight):
    side_count = lax.axis_size("side")
    group_count = lax.axis_size("grp")
    owner_count = lax.axis_size("ex")
    local_experts = gate_weight.shape[0]
    expert_total = local_experts * owner_count
    capacity = tokens.shape[0]
    token_count = tokens.shape[0]
    top_count = expert_ids.shape[1]
    half_width = tokens.shape[1]
    local_hidden = gate_weight.shape[2]
    share_hidden = local_hidden // side_count
    rows_total = group_count * owner_count
    flat_ids = expert_ids.reshape(-1)
    onehot = (flat_ids[:, None] == jnp.arange(expert_total, dtype=jnp.int32)[None, :]).astype(
        jnp.int32
    )
    earlier = jnp.cumsum(onehot, axis=0) - onehot
    slot_of = jnp.sum(earlier * onehot, axis=1)
    target = flat_ids * capacity + slot_of
    placed = (
        target[:, None] == jnp.arange(expert_total * capacity, dtype=jnp.int32)[None, :]
    ).astype(jnp.float32)
    placed = placed.reshape(token_count, top_count, expert_total * capacity)
    dispatch = jnp.sum(placed, axis=1).astype(jnp.bfloat16)
    lifted = jax.nn.sigmoid(scores)
    route_weight = 2.5 * lifted / jnp.sum(lifted, axis=-1, keepdims=True)
    combine = jnp.sum(placed * route_weight[:, :, None], axis=1)
    outgoing = lax.dot_general(
        dispatch, tokens, (((0,), (0,)), ((), ())), preferred_element_type=jnp.float32
    )
    outgoing = outgoing.astype(jnp.bfloat16).reshape(
        owner_count, local_experts, capacity, half_width
    )
    paired = jnp.stack(
        [
            gate_weight.reshape(local_experts, half_width, side_count, share_hidden),
            up_weight.reshape(local_experts, half_width, side_count, share_hidden),
        ],
        axis=3,
    )
    paired = paired.reshape(local_experts, half_width, 2 * local_hidden)
    widened = lax.all_gather(
        outgoing.reshape(owner_count, 1, local_experts, capacity, half_width),
        "grp",
        axis=1,
        tiled=True,
    )
    arrived = lax.all_to_all(widened, "ex", split_axis=0, concat_axis=0, tiled=True)
    ordered = jnp.transpose(arrived, (1, 0, 2, 3, 4)).reshape(
        rows_total, local_experts, capacity, half_width
    )
    partial_sums = jnp.einsum("secd,edh->sech", ordered, paired, preferred_element_type=jnp.float32)
    out_width = down_weight.shape[2]
    summed = lax.psum(partial_sums, "side")
    parts = summed.reshape(rows_total, local_experts, capacity, side_count, 2, share_hidden)
    hidden = (jax.nn.silu(parts[..., 0, :]) * parts[..., 1, :]).reshape(
        rows_total, local_experts, capacity, local_hidden
    )
    hidden = hidden.astype(jnp.bfloat16)
    expert_sum = make_fold(down_weight, lax.all_gather(hidden, "grp", axis=3, tiled=True))
    expert_out = expert_sum.astype(jnp.bfloat16).reshape(
        group_count, owner_count, local_experts, capacity, out_width
    )
    by_owner = lax.all_to_all(
        lax.all_to_all(expert_out, "grp", split_axis=0, concat_axis=4, tiled=True),
        "ex",
        split_axis=1,
        concat_axis=1,
        tiled=True,
    )
    returned = by_owner.reshape(expert_total * capacity, half_width).astype(jnp.float32)
    combined = jnp.dot(
        combine, returned, precision=lax.Precision.HIGHEST, preferred_element_type=jnp.float32
    )
    return combined.astype(jnp.bfloat16)


def unpack_matrix(piece, tokens, rows, transposed=False):
    shape = (rows, tokens) if transposed else (tokens, rows)
    token = lax.broadcasted_iota(jnp.int32, shape, 1 if transposed else 0)
    row = lax.broadcasted_iota(jnp.int32, shape, 0 if transposed else 1)
    source = lax.shift_right_logical(token * 171, 9)
    target = (ROWS - TOK) * source + token + TOK * piece
    return jnp.where(row == target, 1.0, 0.0).astype(jnp.bfloat16)


def fused_kernel(
    dims,
    tok_ref,
    ids_ref,
    score_ref,
    gate_hbm,
    up_hbm,
    down_hbm,
    out_ref,
    gate_v,
    up_v,
    down_v,
    pack_f,
    block,
    gathered,
    x_ref,
    mine,
    other,
    hidden,
    acc,
    ret,
    back,
    fin,
    gate_sem,
    up_sem,
    down_sem,
    tok_send,
    tok_recv,
    side_send,
    side_recv,
    hid_send,
    hid_recv,
    ret_send,
    ret_recv,
):
    groups, owners, experts, width, hid, out_w, lanes, ret_lanes = dims
    count = groups * owners
    tokens = count * TOK
    rows = count * ROWS
    side = lax.axis_index("side")
    grp = lax.axis_index("grp")
    own = lax.axis_index("ex")
    me = grp * owners + own
    sibling = {"side": 1 - side}

    def loads(e):
        return (
            pltpu.make_async_copy(gate_hbm.at[e], gate_v.at[e], gate_sem.at[e]),
            pltpu.make_async_copy(up_hbm.at[e], up_v.at[e], up_sem.at[e]),
            pltpu.make_async_copy(down_hbm.at[e], down_v.at[e], down_sem.at[e]),
        )

    for e in range(experts):
        gate_copy, up_copy, _ = loads(e)
        gate_copy.start()
        up_copy.start()
    for e in range(experts):
        loads(e)[2].start()

    def peer(step):
        target = lax.rem(me + step, count)
        return target, {"grp": target // owners, "ex": lax.rem(target, owners)}

    barrier = pltpu.get_barrier_semaphore()
    for step in range(1, count):
        pl.semaphore_signal(
            barrier, inc=1, device_id=peer(step)[1], device_id_type=pl.DeviceIdType.MESH
        )
    pl.semaphore_signal(barrier, inc=1, device_id=sibling, device_id_type=pl.DeviceIdType.MESH)

    lifted = jax.nn.sigmoid(score_ref[...])
    route = 2.5 * lifted / jnp.sum(lifted, axis=-1, keepdims=True)
    ids = ids_ref[...]
    expert_lane = lax.broadcasted_iota(jnp.int32, (TOK, 128), 1)
    dense = jnp.zeros((TOK, 128), jnp.float32)
    for k in range(ids.shape[1]):
        dense = dense + jnp.where(ids[:, k : k + 1] == expert_lane, route[:, k : k + 1], 0.0)
    high = dense.astype(jnp.bfloat16).astype(jnp.float32)
    low = dense - high
    pack_f[...] = jnp.zeros_like(pack_f)
    for piece in range(PACK):
        begin = piece * lanes
        size = min(lanes, width - begin)
        pack_f[pl.ds(TOK * piece, TOK), pl.ds(0, size)] = tok_ref[:, pl.ds(begin, size)].astype(
            jnp.float32
        )
    spare = width - (PACK - 1) * lanes
    pack_f[pl.ds(TOK * (PACK - 1), TOK), pl.ds(spare, 128)] = high
    pack_f[pl.ds(TOK * (PACK - 1), TOK), pl.ds(spare + 128, 128)] = low
    packed = pack_f[...].astype(jnp.bfloat16)
    block[...] = packed
    my_rows = pl.ds(pl.multiple_of(me * ROWS, ROWS), ROWS)
    gathered[my_rows, :] = packed

    pl.semaphore_wait(barrier, count)

    def token_copy(step):
        return pltpu.make_async_remote_copy(
            src_ref=block,
            dst_ref=gathered.at[my_rows],
            send_sem=tok_send.at[step - 1],
            recv_sem=tok_recv.at[step - 1],
            device_id=peer(step)[1],
            device_id_type=pl.DeviceIdType.MESH,
        )

    token_copies = [token_copy(step) for step in range(1, count)]
    for copy in token_copies:
        copy.start()
    for copy in token_copies:
        copy.wait_recv()

    weights = None
    for piece in range(PACK):
        part = jnp.dot(
            unpack_matrix(piece, tokens, rows),
            gathered[...],
            preferred_element_type=jnp.float32,
        )
        size = min(lanes, width - piece * lanes)
        x_ref[:, pl.ds(piece * lanes, size)] = part[:, :size].astype(jnp.bfloat16)
        if piece == PACK - 1:
            weights = part[:, spare : spare + 128] + part[:, spare + 128 : spare + 256]

    def side_copy(e):
        return pltpu.make_async_remote_copy(
            src_ref=mine.at[e],
            dst_ref=other.at[e],
            send_sem=side_send.at[e],
            recv_sem=side_recv.at[e],
            device_id=sibling,
            device_id_type=pl.DeviceIdType.MESH,
        )

    def hidden_copy(e, step):
        return pltpu.make_async_remote_copy(
            src_ref=hidden.at[e, grp],
            dst_ref=hidden.at[e, grp],
            send_sem=hid_send.at[e, step - 1],
            recv_sem=hid_recv.at[e, step - 1],
            device_id={"grp": lax.rem(grp + step, groups)},
            device_id_type=pl.DeviceIdType.MESH,
        )

    def gate_up(e):
        gate_copy, up_copy, _ = loads(e)
        for weight, copy, begin in ((gate_v, gate_copy, 0), (up_v, up_copy, hid)):
            copy.wait()
            mine[e, :, pl.ds(begin, hid)] = jnp.dot(
                x_ref[...], weight[e], preferred_element_type=jnp.float32
            )
        side_copy(e).start()

    def activate(e):
        side_copy(e).wait_recv()
        gate = mine[e, :, pl.ds(0, hid)] + other[e, :, pl.ds(0, hid)]
        up = mine[e, :, pl.ds(hid, hid)] + other[e, :, pl.ds(hid, hid)]
        hidden[e, grp] = (gate / (1.0 + jnp.exp(-gate)) * up).astype(jnp.bfloat16)
        for step in range(1, groups):
            hidden_copy(e, step).start()

    acc[...] = jnp.zeros_like(acc)

    def down(e):
        loads(e)[2].wait()
        for step in range(1, groups):
            hidden_copy(e, step).wait_recv()
        lhs = jnp.concatenate([hidden[e, j] for j in range(groups)], axis=1)
        lane = lax.broadcasted_iota(jnp.int32, weights.shape, 1)
        factor = jnp.sum(
            jnp.where(lane == own * experts + e, weights, 0.0), axis=1, keepdims=True
        )
        for begin in range(0, out_w, 256):
            size = min(256, out_w - begin)
            result = jnp.dot(
                lhs, down_v[e, :, pl.ds(begin, size)], preferred_element_type=jnp.float32
            )
            result = result.astype(jnp.bfloat16).astype(jnp.float32)
            acc[:, pl.ds(begin, size)] += factor * result

    for e in range(experts):
        gate_up(e)
        if e > 0:
            activate(e - 1)
    if experts > 1:
        down(0)
    activate(experts - 1)
    for e in range(1 if experts > 1 else 0, experts):
        down(e)

    packed_out = jnp.zeros((rows, ret_lanes), jnp.float32)
    for piece in range(acc.shape[1] // ret_lanes):
        packed_out = packed_out + jnp.dot(
            unpack_matrix(piece, tokens, rows, True),
            acc[:, pl.ds(piece * ret_lanes, ret_lanes)].astype(jnp.bfloat16),
            preferred_element_type=jnp.float32,
        )
    ret[...] = packed_out.astype(jnp.bfloat16)

    def return_copy(step):
        target, device = peer(step)
        return pltpu.make_async_remote_copy(
            src_ref=ret.at[pl.ds(pl.multiple_of(target * ROWS, ROWS), ROWS)],
            dst_ref=back.at[my_rows],
            send_sem=ret_send.at[step - 1],
            recv_sem=ret_recv.at[step - 1],
            device_id=device,
            device_id_type=pl.DeviceIdType.MESH,
        )

    return_copies = [return_copy(step) for step in range(1, count)]
    for copy in return_copies:
        copy.start()
    back[my_rows, :] = ret[my_rows, :]
    for copy in token_copies:
        copy.wait_send()
    for e in range(experts):
        side_copy(e).wait_send()
        for step in range(1, groups):
            hidden_copy(e, step).wait_send()
    for copy in return_copies:
        copy.wait_recv()
    for j in range(groups):
        total = back[pl.ds(j * owners * ROWS, ROWS), :].astype(jnp.float32)
        for k in range(1, owners):
            total = total + back[pl.ds((j * owners + k) * ROWS, ROWS), :].astype(jnp.float32)
        fin[j] = total
        for piece in range(acc.shape[1] // ret_lanes):
            begin = piece * ret_lanes
            size = min(ret_lanes, out_w - begin)
            out_ref[:, pl.ds(j * out_w + begin, size)] = fin[
                j, pl.ds(TOK * piece, TOK), pl.ds(0, size)
            ].astype(jnp.bfloat16)
    for copy in return_copies:
        copy.wait_send()


def ceil_lanes(size, pieces):
    return -(-size // (128 * pieces)) * 128


def fused(dims, tokens, expert_ids, scores, gate_weight, up_weight, down_weight):
    groups, owners, experts, width, hid, out_w, lanes, ret_lanes = dims
    count = groups * owners
    acc_w = -(-out_w // ret_lanes) * ret_lanes
    rows = count * ROWS
    vmem = pl.BlockSpec(memory_space=pltpu.VMEM)
    hbm = pl.BlockSpec(memory_space=pl.ANY)
    dma = pltpu.SemaphoreType.DMA
    weight_count = gate_weight.size + up_weight.size + down_weight.size
    return pl.pallas_call(
        functools.partial(fused_kernel, dims),
        out_shape=jax.ShapeDtypeStruct(tokens.shape, jnp.bfloat16),
        in_specs=[vmem, vmem, vmem, hbm, hbm, hbm],
        out_specs=vmem,
        scratch_shapes=[
            pltpu.VMEM(gate_weight.shape, jnp.bfloat16),
            pltpu.VMEM(up_weight.shape, jnp.bfloat16),
            pltpu.VMEM(down_weight.shape, jnp.bfloat16),
            pltpu.VMEM((ROWS, lanes), jnp.float32),
            pltpu.VMEM((ROWS, lanes), jnp.bfloat16),
            pltpu.VMEM((rows, lanes), jnp.bfloat16),
            pltpu.VMEM((count * TOK, width), jnp.bfloat16),
            pltpu.VMEM((experts, count * TOK, 2 * hid), jnp.float32),
            pltpu.VMEM((experts, count * TOK, 2 * hid), jnp.float32),
            pltpu.VMEM((experts, groups, count * TOK, hid), jnp.bfloat16),
            pltpu.VMEM((count * TOK, acc_w), jnp.float32),
            pltpu.VMEM((rows, ret_lanes), jnp.bfloat16),
            pltpu.VMEM((rows, ret_lanes), jnp.bfloat16),
            pltpu.VMEM((groups, ROWS, ret_lanes), jnp.float32),
            dma((experts,)),
            dma((experts,)),
            dma((experts,)),
            dma((count - 1,)),
            dma((count - 1,)),
            dma((experts,)),
            dma((experts,)),
            dma((experts, groups - 1)),
            dma((experts, groups - 1)),
            dma((count - 1,)),
            dma((count - 1,)),
        ],
        compiler_params=pltpu.CompilerParams(
            collective_id=0, has_side_effects=True, vmem_limit_bytes=58 * 1024 * 1024
        ),
        cost_estimate=pl.CostEstimate(
            flops=2 * count * TOK * weight_count,
            bytes_accessed=2 * weight_count,
            transcendentals=count * TOK * experts * hid,
        ),
    )(tokens, expert_ids, scores, gate_weight, up_weight, down_weight)


def choose(tokens, expert_ids, scores, gate_weight, up_weight, down_weight):
    groups, owners = lax.axis_size("grp"), lax.axis_size("ex")
    experts, width, hid = gate_weight.shape
    out_w = down_weight.shape[2]
    lanes = ceil_lanes(width + 256, PACK)
    ret_lanes = ceil_lanes(out_w, PACK)
    fits = (
        tokens.shape[0] == TOK
        and lax.axis_size("side") == 2
        and groups > 1
        and groups * owners == 16
        and hid % 128 == 0
        and out_w % 128 == 0
        and width - (PACK - 1) * lanes > 0
        and experts * owners <= 128
        and experts * (2 * width * hid + groups * hid * out_w) * 2 <= 44 * 1024 * 1024
    )
    if not fits:
        return per_device(tokens, expert_ids, scores, gate_weight, up_weight, down_weight)
    dims = (groups, owners, experts, width, hid, out_w, lanes, ret_lanes)
    return fused(dims, tokens, expert_ids, scores, gate_weight, up_weight, down_weight)


def solution(mesh):
    in_specs = (
        P(("grp", "ex"), "side"),
        P(("grp", "ex"), None),
        P(("grp", "ex"), None),
        P("ex", "side", "grp"),
        P("ex", "side", "grp"),
        P("ex", None, ("side", "grp")),
    )
    out_specs = P(("grp", "ex"), "side")
    return jax.shard_map(
        choose, mesh=mesh, in_specs=in_specs, out_specs=out_specs, check_vma=False
    )
```

```python
import functools

import jax
import jax.numpy as jnp
from jax import lax
from jax.experimental import pallas as pl
from jax.experimental.pallas import tpu as pltpu
from jax.sharding import PartitionSpec as P

TOK = 3
ROWS = 16
PACK = ROWS // TOK


def make_fold(table, piece):
    return jnp.einsum("sech,ehd->secd", piece, table, preferred_element_type=jnp.float32)


def per_device(tokens, expert_ids, scores, gate_weight, up_weight, down_weight):
    side_count = lax.axis_size("side")
    group_count = lax.axis_size("grp")
    owner_count = lax.axis_size("ex")
    local_experts = gate_weight.shape[0]
    expert_total = local_experts * owner_count
    capacity = tokens.shape[0]
    token_count = tokens.shape[0]
    top_count = expert_ids.shape[1]
    half_width = tokens.shape[1]
    local_hidden = gate_weight.shape[2]
    share_hidden = local_hidden // side_count
    rows_total = group_count * owner_count
    flat_ids = expert_ids.reshape(-1)
    onehot = (flat_ids[:, None] == jnp.arange(expert_total, dtype=jnp.int32)[None, :]).astype(
        jnp.int32
    )
    earlier = jnp.cumsum(onehot, axis=0) - onehot
    slot_of = jnp.sum(earlier * onehot, axis=1)
    target = flat_ids * capacity + slot_of
    placed = (
        target[:, None] == jnp.arange(expert_total * capacity, dtype=jnp.int32)[None, :]
    ).astype(jnp.float32)
    placed = placed.reshape(token_count, top_count, expert_total * capacity)
    dispatch = jnp.sum(placed, axis=1).astype(jnp.bfloat16)
    lifted = jax.nn.sigmoid(scores)
    route_weight = 2.5 * lifted / jnp.sum(lifted, axis=-1, keepdims=True)
    combine = jnp.sum(placed * route_weight[:, :, None], axis=1)
    outgoing = lax.dot_general(
        dispatch, tokens, (((0,), (0,)), ((), ())), preferred_element_type=jnp.float32
    )
    outgoing = outgoing.astype(jnp.bfloat16).reshape(
        owner_count, local_experts, capacity, half_width
    )
    paired = jnp.stack(
        [
            gate_weight.reshape(local_experts, half_width, side_count, share_hidden),
            up_weight.reshape(local_experts, half_width, side_count, share_hidden),
        ],
        axis=3,
    )
    paired = paired.reshape(local_experts, half_width, 2 * local_hidden)
    widened = lax.all_gather(
        outgoing.reshape(owner_count, 1, local_experts, capacity, half_width),
        "grp",
        axis=1,
        tiled=True,
    )
    arrived = lax.all_to_all(widened, "ex", split_axis=0, concat_axis=0, tiled=True)
    ordered = jnp.transpose(arrived, (1, 0, 2, 3, 4)).reshape(
        rows_total, local_experts, capacity, half_width
    )
    partial_sums = jnp.einsum("secd,edh->sech", ordered, paired, preferred_element_type=jnp.float32)
    out_width = down_weight.shape[2]
    summed = lax.psum(partial_sums, "side")
    parts = summed.reshape(rows_total, local_experts, capacity, side_count, 2, share_hidden)
    hidden = (jax.nn.silu(parts[..., 0, :]) * parts[..., 1, :]).reshape(
        rows_total, local_experts, capacity, local_hidden
    )
    hidden = hidden.astype(jnp.bfloat16)
    expert_sum = make_fold(down_weight, lax.all_gather(hidden, "grp", axis=3, tiled=True))
    expert_out = expert_sum.astype(jnp.bfloat16).reshape(
        group_count, owner_count, local_experts, capacity, out_width
    )
    by_owner = lax.all_to_all(
        lax.all_to_all(expert_out, "grp", split_axis=0, concat_axis=4, tiled=True),
        "ex",
        split_axis=1,
        concat_axis=1,
        tiled=True,
    )
    returned = by_owner.reshape(expert_total * capacity, half_width).astype(jnp.float32)
    combined = jnp.dot(
        combine, returned, precision=lax.Precision.HIGHEST, preferred_element_type=jnp.float32
    )
    return combined.astype(jnp.bfloat16)


def unpack_matrix(piece, tokens, rows, transposed=False):
    shape = (rows, tokens) if transposed else (tokens, rows)
    token = lax.broadcasted_iota(jnp.int32, shape, 1 if transposed else 0)
    row = lax.broadcasted_iota(jnp.int32, shape, 0 if transposed else 1)
    source = lax.shift_right_logical(token * 171, 9)
    target = (ROWS - TOK) * source + token + TOK * piece
    return jnp.where(row == target, 1.0, 0.0).astype(jnp.bfloat16)


def fused_kernel(
    dims,
    tok_hbm,
    ids_hbm,
    score_hbm,
    gate_hbm,
    up_hbm,
    down_hbm,
    out_ref,
    tok_ref,
    ids_ref,
    score_ref,
    gate_v,
    up_v,
    down_v,
    pack_f,
    block,
    gathered,
    x_ref,
    mine,
    other,
    hidden,
    acc,
    ret,
    back,
    fin,
    in_sem,
    gate_sem,
    up_sem,
    down_sem,
    tok_send,
    tok_recv,
    side_send,
    side_recv,
    hid_send,
    hid_recv,
    ret_send,
    ret_recv,
):
    groups, owners, experts, width, hid, out_w, lanes = dims
    count = groups * owners
    tokens = count * TOK
    rows = count * ROWS
    span = PACK * lanes
    cut = span // 256 * 256
    early = min(2, experts)
    side = lax.axis_index("side")
    grp = lax.axis_index("grp")
    own = lax.axis_index("ex")
    me = grp * owners + own
    sibling = {"side": 1 - side}
    mesh_id = pl.DeviceIdType.MESH

    inputs = [
        pltpu.make_async_copy(source, target, in_sem.at[i])
        for i, (source, target) in enumerate(
            ((tok_hbm, tok_ref), (ids_hbm, ids_ref), (score_hbm, score_ref))
        )
    ]
    for copy in inputs:
        copy.start()

    def gate_up_loads(e, half):
        part = pl.ds(0, cut) if half == 0 else pl.ds(cut, width - cut)
        return (
            pltpu.make_async_copy(
                gate_hbm.at[e, part], gate_v.at[e, part], gate_sem.at[e, half]
            ),
            pltpu.make_async_copy(up_hbm.at[e, part], up_v.at[e, part], up_sem.at[e, half]),
        )

    def down_load(e):
        return pltpu.make_async_copy(down_hbm.at[e], down_v.at[e], down_sem.at[e])

    order = [(e, 0) for e in range(early)] + [(e, 1) for e in range(early)]
    order += [(e, half) for e in range(early, experts) for half in range(2)]
    for e, half in order:
        for copy in gate_up_loads(e, half):
            copy.start()
    for e in range(experts):
        down_load(e).start()

    def peer(step):
        target = lax.rem(me + step, count)
        return target, {"grp": target // owners, "ex": lax.rem(target, owners)}

    barrier = pltpu.get_barrier_semaphore()
    for step in range(1, count):
        pl.semaphore_signal(barrier, inc=1, device_id=peer(step)[1], device_id_type=mesh_id)
    pl.semaphore_signal(barrier, inc=1, device_id=sibling, device_id_type=mesh_id)

    pack_f[...] = jnp.zeros_like(pack_f)
    for copy in inputs:
        copy.wait()
    lifted = jax.nn.sigmoid(score_ref[...])
    route = 2.5 * lifted / jnp.sum(lifted, axis=-1, keepdims=True)
    ids = ids_ref[...]
    expert_lane = lax.broadcasted_iota(jnp.int32, (TOK, 128), 1)
    dense = jnp.zeros((TOK, 128), jnp.float32)
    for k in range(ids.shape[1]):
        dense = dense + jnp.where(ids[:, k : k + 1] == expert_lane, route[:, k : k + 1], 0.0)
    high = dense.astype(jnp.bfloat16).astype(jnp.float32)
    low = dense - high
    spare = width - (2 * PACK - 1) * lanes
    my_rows = pl.ds(pl.multiple_of(me * ROWS, ROWS), ROWS)
    for half in range(2):
        for piece in range(PACK):
            begin = half * span + piece * lanes
            size = min(lanes, width - begin)
            pack_f[half, pl.ds(TOK * piece, TOK), pl.ds(0, size)] = tok_ref[
                :, pl.ds(begin, size)
            ].astype(jnp.float32)
        if half == 1:
            last = pl.ds(TOK * (PACK - 1), TOK)
            pack_f[half, last, pl.ds(spare, 128)] = high
            pack_f[half, last, pl.ds(spare + 128, 128)] = low
        packed = pack_f[half].astype(jnp.bfloat16)
        block[half] = packed
        gathered[half, my_rows, :] = packed

    pl.semaphore_wait(barrier, count)

    def flip(bits):
        value = own
        for bit in (1, 2):
            if bits & bit:
                value = value + bit - 2 * bit * lax.rem(value // bit, 2)
        return value

    def token_copy(half, along_grp, along_ex):
        if along_grp and along_ex:
            start_row = (grp * owners + flip(along_ex)) * ROWS
            place = pl.ds(pl.multiple_of(start_row, ROWS), ROWS)
            source = gathered.at[half, place]
        else:
            place = my_rows
            source = block.at[half]
        device = (
            {"grp": lax.rem(grp + along_grp, groups)} if along_grp else {"ex": flip(along_ex)}
        )
        return pltpu.make_async_remote_copy(
            src_ref=source,
            dst_ref=gathered.at[half, place],
            send_sem=tok_send.at[half, along_grp, along_ex],
            recv_sem=tok_recv.at[half, along_grp, along_ex],
            device_id=device,
            device_id_type=mesh_id,
        )

    for half in range(2):
        for along_ex in range(1, owners):
            token_copy(half, 0, along_ex).start()
    for half in range(2):
        for along_grp in range(1, groups):
            token_copy(half, along_grp, 0).start()
        for along_ex in range(1, owners):
            token_copy(half, 0, along_ex).wait_recv()
            for along_grp in range(1, groups):
                token_copy(half, along_grp, along_ex).start()

    acc[...] = jnp.zeros_like(acc)
    picks = [unpack_matrix(piece, tokens, rows) for piece in range(PACK)]

    def unpack(half):
        for along_grp in range(1, groups):
            for along_ex in range(owners):
                token_copy(half, along_grp, along_ex).wait_recv()
        for piece in range(PACK):
            part = jnp.dot(picks[piece], gathered[half], preferred_element_type=jnp.float32)
            begin = half * span + piece * lanes
            size = min(lanes, width - begin)
            x_ref[:, pl.ds(begin, size)] = part[:, :size].astype(jnp.bfloat16)
        return part[:, spare : spare + 128] + part[:, spare + 128 : spare + 256]

    def side_copy(e):
        return pltpu.make_async_remote_copy(
            src_ref=mine.at[e],
            dst_ref=other.at[e],
            send_sem=side_send.at[e],
            recv_sem=side_recv.at[e],
            device_id=sibling,
            device_id_type=mesh_id,
        )

    def hidden_copy(e, step):
        return pltpu.make_async_remote_copy(
            src_ref=hidden.at[e, grp],
            dst_ref=hidden.at[e, grp],
            send_sem=hid_send.at[e, step - 1],
            recv_sem=hid_recv.at[e, step - 1],
            device_id={"grp": lax.rem(grp + step, groups)},
            device_id_type=mesh_id,
        )

    def gate_up_first(e):
        for i, weight in enumerate((gate_v, up_v)):
            gate_up_loads(e, 0)[i].wait()
            mine[e, :, pl.ds(i * hid, hid)] = jnp.dot(
                x_ref[:, pl.ds(0, cut)],
                weight[e, pl.ds(0, cut)],
                preferred_element_type=jnp.float32,
            )

    def gate_up_rest(e):
        for i, weight in enumerate((gate_v, up_v)):
            gate_up_loads(e, 1)[i].wait()
            if e < early:
                mine[e, :, pl.ds(i * hid, hid)] += jnp.dot(
                    x_ref[:, pl.ds(cut, width - cut)],
                    weight[e, pl.ds(cut, width - cut)],
                    preferred_element_type=jnp.float32,
                )
            else:
                gate_up_loads(e, 0)[i].wait()
                mine[e, :, pl.ds(i * hid, hid)] = jnp.dot(
                    x_ref[...], weight[e], preferred_element_type=jnp.float32
                )
        side_copy(e).start()

    def activate(e):
        side_copy(e).wait_recv()
        gate = mine[e, :, pl.ds(0, hid)] + other[e, :, pl.ds(0, hid)]
        up = mine[e, :, pl.ds(hid, hid)] + other[e, :, pl.ds(hid, hid)]
        hidden[e, grp] = (gate / (1.0 + jnp.exp(-gate)) * up).astype(jnp.bfloat16)
        for step in range(1, groups):
            hidden_copy(e, step).start()

    pieces = out_w // 128
    halves = ((0, -(-pieces // 2)), (-(-pieces // 2), pieces))

    def down(e, half):
        if half == 0:
            down_load(e).wait()
            for step in range(1, groups):
                hidden_copy(e, step).wait_recv()
        lhs = jnp.concatenate([hidden[e, j] for j in range(groups)], axis=1)
        lane = lax.broadcasted_iota(jnp.int32, weights.shape, 1)
        factor = jnp.sum(
            jnp.where(lane == own * experts + e, weights, 0.0), axis=1, keepdims=True
        )
        first, stop = halves[half]
        for begin in range(first * 128, stop * 128, 256):
            size = min(256, stop * 128 - begin)
            result = jnp.dot(
                lhs, down_v[e, :, pl.ds(begin, size)], preferred_element_type=jnp.float32
            )
            result = result.astype(jnp.bfloat16).astype(jnp.float32)
            acc[:, pl.ds(begin, size)] += factor * result

    def return_copy(half, step):
        target, device = peer(step)
        return pltpu.make_async_remote_copy(
            src_ref=ret.at[half, pl.ds(pl.multiple_of(target * ROWS, ROWS), ROWS)],
            dst_ref=back.at[half, my_rows],
            send_sem=ret_send.at[half, step - 1],
            recv_sem=ret_recv.at[half, step - 1],
            device_id=device,
            device_id_type=mesh_id,
        )

    def send_back(half):
        first, stop = halves[half]
        packed_out = jnp.zeros((rows, 128), jnp.float32)
        for piece in range(first, stop):
            packed_out = packed_out + jnp.dot(
                unpack_matrix(piece - first, tokens, rows, True),
                acc[:, pl.ds(piece * 128, 128)].astype(jnp.bfloat16),
                preferred_element_type=jnp.float32,
            )
        ret[half] = packed_out.astype(jnp.bfloat16)
        for step in range(1, count):
            return_copy(half, step).start()
        back[half, my_rows, :] = ret[half, my_rows, :]

    unpack(0)
    for e in range(early):
        gate_up_first(e)
    weights = unpack(1)
    for e in range(experts):
        gate_up_rest(e)
        if e > 0:
            activate(e - 1)
    if experts > 1:
        down(0, 0)
    activate(experts - 1)
    if experts > 1:
        down(0, 1)
    for e in range(1, experts - 1):
        down(e, 0)
    for e in range(1, experts - 2):
        down(e, 1)
    down(experts - 1, 0)
    send_back(0)
    for e in range(max(1, experts - 2), experts):
        down(e, 1)
    send_back(1)

    for half in range(2):
        for along_ex in range(1, owners):
            token_copy(half, 0, along_ex).wait_send()
        for along_grp in range(1, groups):
            for along_ex in range(owners):
                token_copy(half, along_grp, along_ex).wait_send()
    for e in range(experts):
        side_copy(e).wait_send()
        for step in range(1, groups):
            hidden_copy(e, step).wait_send()
    for half in range(2):
        for step in range(1, count):
            return_copy(half, step).wait_recv()
        first, stop = halves[half]
        for j in range(groups):
            total = back[half, pl.ds(j * owners * ROWS, ROWS), :].astype(jnp.float32)
            for k in range(1, owners):
                place = pl.ds((j * owners + k) * ROWS, ROWS)
                total = total + back[half, place, :].astype(jnp.float32)
            fin[half, j] = total
            for piece in range(first, stop):
                out_ref[:, pl.ds(j * out_w + piece * 128, 128)] = fin[
                    half, j, pl.ds(TOK * (piece - first), TOK), :
                ].astype(jnp.bfloat16)
    for half in range(2):
        for step in range(1, count):
            return_copy(half, step).wait_send()


def ceil_lanes(size, pieces):
    return -(-size // (128 * pieces)) * 128


def fused(dims, tokens, expert_ids, scores, gate_weight, up_weight, down_weight):
    groups, owners, experts, width, hid, out_w, lanes = dims
    count = groups * owners
    rows = count * ROWS
    vmem = pl.BlockSpec(memory_space=pltpu.VMEM)
    hbm = pl.BlockSpec(memory_space=pl.ANY)
    dma = pltpu.SemaphoreType.DMA
    weight_count = gate_weight.size + up_weight.size + down_weight.size
    return pl.pallas_call(
        functools.partial(fused_kernel, dims),
        out_shape=jax.ShapeDtypeStruct(tokens.shape, jnp.bfloat16),
        in_specs=[hbm] * 6,
        out_specs=vmem,
        scratch_shapes=[
            pltpu.VMEM(tokens.shape, jnp.bfloat16),
            pltpu.VMEM(expert_ids.shape, jnp.int32),
            pltpu.VMEM(scores.shape, jnp.float32),
            pltpu.VMEM(gate_weight.shape, jnp.bfloat16),
            pltpu.VMEM(up_weight.shape, jnp.bfloat16),
            pltpu.VMEM(down_weight.shape, jnp.bfloat16),
            pltpu.VMEM((2, ROWS, lanes), jnp.float32),
            pltpu.VMEM((2, ROWS, lanes), jnp.bfloat16),
            pltpu.VMEM((2, rows, lanes), jnp.bfloat16),
            pltpu.VMEM((count * TOK, width), jnp.bfloat16),
            pltpu.VMEM((experts, count * TOK, 2 * hid), jnp.float32),
            pltpu.VMEM((experts, count * TOK, 2 * hid), jnp.float32),
            pltpu.VMEM((experts, groups, count * TOK, hid), jnp.bfloat16),
            pltpu.VMEM((count * TOK, out_w), jnp.float32),
            pltpu.VMEM((2, rows, 128), jnp.bfloat16),
            pltpu.VMEM((2, rows, 128), jnp.bfloat16),
            pltpu.VMEM((2, groups, ROWS, 128), jnp.float32),
            dma((3,)),
            dma((experts, 2)),
            dma((experts, 2)),
            dma((experts,)),
            dma((2, groups, owners)),
            dma((2, groups, owners)),
            dma((experts,)),
            dma((experts,)),
            dma((experts, groups - 1)),
            dma((experts, groups - 1)),
            dma((2, count - 1)),
            dma((2, count - 1)),
        ],
        compiler_params=pltpu.CompilerParams(
            collective_id=0, has_side_effects=True, vmem_limit_bytes=58 * 1024 * 1024
        ),
        cost_estimate=pl.CostEstimate(
            flops=2 * count * TOK * weight_count,
            bytes_accessed=2 * weight_count,
            transcendentals=count * TOK * experts * hid,
        ),
    )(tokens, expert_ids, scores, gate_weight, up_weight, down_weight)


def choose(tokens, expert_ids, scores, gate_weight, up_weight, down_weight):
    groups, owners = lax.axis_size("grp"), lax.axis_size("ex")
    experts, width, hid = gate_weight.shape
    out_w = down_weight.shape[2]
    lanes = ceil_lanes(width + 256, 2 * PACK)
    fits = (
        tokens.shape[0] == TOK
        and lax.axis_size("side") == 2
        and groups == 4
        and owners == 4
        and hid % 128 == 0
        and out_w % 128 == 0
        and 256 <= out_w <= 2 * PACK * 128
        and width % 128 == 0
        and width - (2 * PACK - 1) * lanes > 0
        and experts * owners <= 128
        and experts * (2 * width * hid + groups * hid * out_w) * 2 <= 44 * 1024 * 1024
    )
    if not fits:
        return per_device(tokens, expert_ids, scores, gate_weight, up_weight, down_weight)
    dims = (groups, owners, experts, width, hid, out_w, lanes)
    return fused(dims, tokens, expert_ids, scores, gate_weight, up_weight, down_weight)


def solution(mesh):
    in_specs = (
        P(("grp", "ex"), "side"),
        P(("grp", "ex"), None),
        P(("grp", "ex"), None),
        P("ex", "side", "grp"),
        P("ex", "side", "grp"),
        P("ex", None, ("side", "grp")),
    )
    out_specs = P(("grp", "ex"), "side")
    return jax.shard_map(
        choose, mesh=mesh, in_specs=in_specs, out_specs=out_specs, check_vma=False
    )
```

```python
import functools

import jax
import jax.numpy as jnp
from jax import lax
from jax.experimental import pallas as pl
from jax.experimental.pallas import tpu as pltpu
from jax.sharding import PartitionSpec as P

TOK = 3
ROWS = 16
PACK = ROWS // TOK


def make_fold(table, piece):
    return jnp.einsum("sech,ehd->secd", piece, table, preferred_element_type=jnp.float32)


def per_device(tokens, expert_ids, scores, gate_weight, up_weight, down_weight):
    side_count = lax.axis_size("side")
    group_count = lax.axis_size("grp")
    owner_count = lax.axis_size("ex")
    local_experts = gate_weight.shape[0]
    expert_total = local_experts * owner_count
    capacity = tokens.shape[0]
    token_count = tokens.shape[0]
    top_count = expert_ids.shape[1]
    half_width = tokens.shape[1]
    local_hidden = gate_weight.shape[2]
    share_hidden = local_hidden // side_count
    rows_total = group_count * owner_count
    flat_ids = expert_ids.reshape(-1)
    onehot = (flat_ids[:, None] == jnp.arange(expert_total, dtype=jnp.int32)[None, :]).astype(
        jnp.int32
    )
    earlier = jnp.cumsum(onehot, axis=0) - onehot
    slot_of = jnp.sum(earlier * onehot, axis=1)
    target = flat_ids * capacity + slot_of
    placed = (
        target[:, None] == jnp.arange(expert_total * capacity, dtype=jnp.int32)[None, :]
    ).astype(jnp.float32)
    placed = placed.reshape(token_count, top_count, expert_total * capacity)
    dispatch = jnp.sum(placed, axis=1).astype(jnp.bfloat16)
    lifted = jax.nn.sigmoid(scores)
    route_weight = 2.5 * lifted / jnp.sum(lifted, axis=-1, keepdims=True)
    combine = jnp.sum(placed * route_weight[:, :, None], axis=1)
    outgoing = lax.dot_general(
        dispatch, tokens, (((0,), (0,)), ((), ())), preferred_element_type=jnp.float32
    )
    outgoing = outgoing.astype(jnp.bfloat16).reshape(
        owner_count, local_experts, capacity, half_width
    )
    paired = jnp.stack(
        [
            gate_weight.reshape(local_experts, half_width, side_count, share_hidden),
            up_weight.reshape(local_experts, half_width, side_count, share_hidden),
        ],
        axis=3,
    )
    paired = paired.reshape(local_experts, half_width, 2 * local_hidden)
    widened = lax.all_gather(
        outgoing.reshape(owner_count, 1, local_experts, capacity, half_width),
        "grp",
        axis=1,
        tiled=True,
    )
    arrived = lax.all_to_all(widened, "ex", split_axis=0, concat_axis=0, tiled=True)
    ordered = jnp.transpose(arrived, (1, 0, 2, 3, 4)).reshape(
        rows_total, local_experts, capacity, half_width
    )
    partial_sums = jnp.einsum("secd,edh->sech", ordered, paired, preferred_element_type=jnp.float32)
    out_width = down_weight.shape[2]
    summed = lax.psum(partial_sums, "side")
    parts = summed.reshape(rows_total, local_experts, capacity, side_count, 2, share_hidden)
    hidden = (jax.nn.silu(parts[..., 0, :]) * parts[..., 1, :]).reshape(
        rows_total, local_experts, capacity, local_hidden
    )
    hidden = hidden.astype(jnp.bfloat16)
    expert_sum = make_fold(down_weight, lax.all_gather(hidden, "grp", axis=3, tiled=True))
    expert_out = expert_sum.astype(jnp.bfloat16).reshape(
        group_count, owner_count, local_experts, capacity, out_width
    )
    by_owner = lax.all_to_all(
        lax.all_to_all(expert_out, "grp", split_axis=0, concat_axis=4, tiled=True),
        "ex",
        split_axis=1,
        concat_axis=1,
        tiled=True,
    )
    returned = by_owner.reshape(expert_total * capacity, half_width).astype(jnp.float32)
    combined = jnp.dot(
        combine, returned, precision=lax.Precision.HIGHEST, preferred_element_type=jnp.float32
    )
    return combined.astype(jnp.bfloat16)


def unpack_matrix(piece, tokens, rows, transposed=False):
    shape = (rows, tokens) if transposed else (tokens, rows)
    token = lax.broadcasted_iota(jnp.int32, shape, 1 if transposed else 0)
    row = lax.broadcasted_iota(jnp.int32, shape, 0 if transposed else 1)
    source = lax.shift_right_logical(token * 171, 9)
    target = (ROWS - TOK) * source + token + TOK * piece
    return jnp.where(row == target, 1.0, 0.0).astype(jnp.bfloat16)


def fused_kernel(
    dims,
    tok_hbm,
    ids_hbm,
    score_hbm,
    gate_hbm,
    up_hbm,
    down_hbm,
    out_ref,
    tok_ref,
    ids_ref,
    score_ref,
    gate_v,
    up_v,
    down_v,
    pack_f,
    block,
    gathered,
    x_ref,
    mine,
    other,
    hidden,
    acc,
    ret,
    back,
    ret_grp,
    back_grp,
    in_sem,
    gate_sem,
    up_sem,
    down_sem,
    tok_send,
    tok_recv,
    side_send,
    side_recv,
    hid_send,
    hid_recv,
    ret_send,
    ret_recv,
    last_send,
    last_recv,
):
    groups, owners, experts, width, hid, out_w, lanes, ret_lanes = dims
    count = groups * owners
    tokens = count * TOK
    rows = count * ROWS
    side = lax.axis_index("side")
    grp = lax.axis_index("grp")
    own = lax.axis_index("ex")
    me = grp * owners + own
    sibling = {"side": 1 - side}

    def loads(e):
        return (
            pltpu.make_async_copy(gate_hbm.at[e], gate_v.at[e], gate_sem.at[e]),
            pltpu.make_async_copy(up_hbm.at[e], up_v.at[e], up_sem.at[e]),
            pltpu.make_async_copy(down_hbm.at[e], down_v.at[e], down_sem.at[e]),
        )

    mesh_id = pl.DeviceIdType.MESH
    along_ex = [{"ex": lax.rem(own + step, owners)} for step in range(1, owners)]
    along_grp = [{"grp": lax.rem(grp + step, groups)} for step in range(1, groups)]
    partners = along_ex + along_grp + [sibling]
    inputs = [
        pltpu.make_async_copy(source, target, in_sem.at[i])
        for i, (source, target) in enumerate(
            ((tok_hbm, tok_ref), (ids_hbm, ids_ref), (score_hbm, score_ref))
        )
    ]
    for copy in inputs:
        copy.start()
    barrier = pltpu.get_barrier_semaphore()
    for device in partners:
        pl.semaphore_signal(barrier, inc=1, device_id=device, device_id_type=mesh_id)
    for e in range(experts):
        gate_copy, up_copy, _ = loads(e)
        gate_copy.start()
        up_copy.start()
    for e in range(experts):
        loads(e)[2].start()
    for copy in inputs:
        copy.wait()

    lifted = jax.nn.sigmoid(score_ref[...])
    route = 2.5 * lifted / jnp.sum(lifted, axis=-1, keepdims=True)
    ids = ids_ref[...]
    expert_lane = lax.broadcasted_iota(jnp.int32, (TOK, 128), 1)
    dense = jnp.zeros((TOK, 128), jnp.float32)
    for k in range(ids.shape[1]):
        dense = dense + jnp.where(ids[:, k : k + 1] == expert_lane, route[:, k : k + 1], 0.0)
    high = dense.astype(jnp.bfloat16).astype(jnp.float32)
    low = dense - high
    pack_f[...] = jnp.zeros_like(pack_f)
    for piece in range(PACK):
        begin = piece * lanes
        size = min(lanes, width - begin)
        pack_f[pl.ds(TOK * piece, TOK), pl.ds(0, size)] = tok_ref[:, pl.ds(begin, size)].astype(
            jnp.float32
        )
    spare = width - (PACK - 1) * lanes
    pack_f[pl.ds(TOK * (PACK - 1), TOK), pl.ds(spare, 128)] = high
    pack_f[pl.ds(TOK * (PACK - 1), TOK), pl.ds(spare + 128, 128)] = low
    packed = pack_f[...].astype(jnp.bfloat16)
    block[...] = packed
    my_rows = pl.ds(pl.multiple_of(me * ROWS, ROWS), ROWS)
    gathered[my_rows, :] = packed

    pl.semaphore_wait(barrier, len(partners))

    line = pl.ds(pl.multiple_of(grp * owners * ROWS, owners * ROWS), owners * ROWS)
    ex_copies = [
        pltpu.make_async_remote_copy(
            src_ref=block,
            dst_ref=gathered.at[my_rows],
            send_sem=tok_send.at[i],
            recv_sem=tok_recv.at[i],
            device_id=device,
            device_id_type=mesh_id,
        )
        for i, device in enumerate(along_ex)
    ]
    grp_copies = [
        pltpu.make_async_remote_copy(
            src_ref=gathered.at[line],
            dst_ref=gathered.at[line],
            send_sem=tok_send.at[owners - 1 + i],
            recv_sem=tok_recv.at[owners - 1 + i],
            device_id=device,
            device_id_type=mesh_id,
        )
        for i, device in enumerate(along_grp)
    ]
    for copy in ex_copies:
        copy.start()
    acc[...] = jnp.zeros_like(acc)
    for copy in ex_copies:
        copy.wait_recv()
    for copy in grp_copies:
        copy.start()
    for copy in grp_copies:
        copy.wait_recv()

    weights = None
    for piece in range(PACK):
        part = jnp.dot(
            unpack_matrix(piece, tokens, rows),
            gathered[...],
            preferred_element_type=jnp.float32,
        )
        size = min(lanes, width - piece * lanes)
        x_ref[:, pl.ds(piece * lanes, size)] = part[:, :size].astype(jnp.bfloat16)
        if piece == PACK - 1:
            weights = part[:, spare : spare + 128] + part[:, spare + 128 : spare + 256]

    def side_copy(e):
        return pltpu.make_async_remote_copy(
            src_ref=mine.at[e],
            dst_ref=other.at[e],
            send_sem=side_send.at[e],
            recv_sem=side_recv.at[e],
            device_id=sibling,
            device_id_type=pl.DeviceIdType.MESH,
        )

    def hidden_copy(e, step):
        return pltpu.make_async_remote_copy(
            src_ref=hidden.at[e, grp],
            dst_ref=hidden.at[e, grp],
            send_sem=hid_send.at[e, step - 1],
            recv_sem=hid_recv.at[e, step - 1],
            device_id={"grp": lax.rem(grp + step, groups)},
            device_id_type=pl.DeviceIdType.MESH,
        )

    def gate_up(e):
        gate_copy, up_copy, _ = loads(e)
        for weight, copy, begin in ((gate_v, gate_copy, 0), (up_v, up_copy, hid)):
            copy.wait()
            mine[e, :, pl.ds(begin, hid)] = jnp.dot(
                x_ref[...], weight[e], preferred_element_type=jnp.float32
            )
        side_copy(e).start()

    def activate(e):
        side_copy(e).wait_recv()
        gate = mine[e, :, pl.ds(0, hid)] + other[e, :, pl.ds(0, hid)]
        up = mine[e, :, pl.ds(hid, hid)] + other[e, :, pl.ds(hid, hid)]
        hidden[e, grp] = (gate / (1.0 + jnp.exp(-gate)) * up).astype(jnp.bfloat16)
        for step in range(1, groups):
            hidden_copy(e, step).start()

    def down(e):
        loads(e)[2].wait()
        for step in range(1, groups):
            hidden_copy(e, step).wait_recv()
        lhs = jnp.concatenate([hidden[e, j] for j in range(groups)], axis=1)
        lane = lax.broadcasted_iota(jnp.int32, weights.shape, 1)
        factor = jnp.sum(
            jnp.where(lane == own * experts + e, weights, 0.0), axis=1, keepdims=True
        )
        for begin in range(0, out_w, 256):
            size = min(256, out_w - begin)
            result = jnp.dot(
                lhs, down_v[e, :, pl.ds(begin, size)], preferred_element_type=jnp.float32
            )
            result = result.astype(jnp.bfloat16).astype(jnp.float32)
            acc[:, pl.ds(begin, size)] += factor * result

    for e in range(experts):
        gate_up(e)
        if e > 0:
            activate(e - 1)
    if experts > 1:
        down(0)
    activate(experts - 1)
    for e in range(1 if experts > 1 else 0, experts):
        down(e)

    line_rows = owners * ROWS
    token = lax.broadcasted_iota(jnp.int32, (line_rows, tokens), 1)
    row = lax.broadcasted_iota(jnp.int32, (line_rows, tokens), 0)
    source = lax.shift_right_logical(token * 171, 9)
    source_grp = sum((source >= owners * j).astype(jnp.int32) for j in range(1, groups))
    target = (source - owners * source_grp) * ROWS + TOK * source_grp + (token - TOK * source)
    by_owner = jnp.where(row == target, 1.0, 0.0).astype(jnp.bfloat16)
    ret[...] = jnp.dot(
        by_owner, acc[:, pl.ds(0, out_w)].astype(jnp.bfloat16), preferred_element_type=jnp.float32
    ).astype(jnp.bfloat16)

    def owner_rows(index):
        return pl.ds(pl.multiple_of(index * ROWS, ROWS), ROWS)

    return_copies = [
        pltpu.make_async_remote_copy(
            src_ref=ret.at[owner_rows(device["ex"])],
            dst_ref=back.at[owner_rows(own)],
            send_sem=ret_send.at[i],
            recv_sem=ret_recv.at[i],
            device_id=device,
            device_id_type=mesh_id,
        )
        for i, device in enumerate(along_ex)
    ]
    for copy in return_copies:
        copy.start()
    back[owner_rows(own), :] = ret[owner_rows(own), :]
    for copy in ex_copies + grp_copies:
        copy.wait_send()
    for e in range(experts):
        side_copy(e).wait_send()
        for step in range(1, groups):
            hidden_copy(e, step).wait_send()
    for copy in return_copies:
        copy.wait_recv()
    total = back[pl.ds(0, ROWS), :].astype(jnp.float32)
    for k in range(1, owners):
        total = total + back[pl.ds(k * ROWS, ROWS), :].astype(jnp.float32)
    total = total.astype(jnp.bfloat16)
    if acc.shape[1] > out_w:
        spread = jnp.zeros((ROWS, acc.shape[1] - out_w), jnp.bfloat16)
        total = jnp.concatenate([total, spread], axis=1)
    packed_out = jnp.zeros((groups * ROWS, ret_lanes), jnp.float32)
    for piece in range(acc.shape[1] // ret_lanes):
        packed_out = packed_out + jnp.dot(
            unpack_matrix(piece, ROWS, groups * ROWS, True),
            total[:, piece * ret_lanes : (piece + 1) * ret_lanes],
            preferred_element_type=jnp.float32,
        )
    ret_grp[...] = packed_out.astype(jnp.bfloat16)
    last_copies = [
        pltpu.make_async_remote_copy(
            src_ref=ret_grp.at[owner_rows(device["grp"])],
            dst_ref=back_grp.at[owner_rows(grp)],
            send_sem=last_send.at[i],
            recv_sem=last_recv.at[i],
            device_id=device,
            device_id_type=mesh_id,
        )
        for i, device in enumerate(along_grp)
    ]
    for copy in last_copies:
        copy.start()
    back_grp[owner_rows(grp), :] = ret_grp[owner_rows(grp), :]
    for copy in return_copies:
        copy.wait_send()
    for copy in last_copies:
        copy.wait_recv()
    for j in range(groups):
        final = back_grp[pl.ds(j * ROWS, ROWS), :].astype(jnp.float32)
        for piece in range(acc.shape[1] // ret_lanes):
            begin = piece * ret_lanes
            size = min(ret_lanes, out_w - begin)
            out_ref[:, pl.ds(j * out_w + begin, size)] = final[
                TOK * piece : TOK * (piece + 1), :size
            ].astype(jnp.bfloat16)
    for copy in last_copies:
        copy.wait_send()


def ceil_lanes(size, pieces):
    return -(-size // (128 * pieces)) * 128


def fused(dims, tokens, expert_ids, scores, gate_weight, up_weight, down_weight):
    groups, owners, experts, width, hid, out_w, lanes, ret_lanes = dims
    count = groups * owners
    acc_w = -(-out_w // ret_lanes) * ret_lanes
    rows = count * ROWS
    vmem = pl.BlockSpec(memory_space=pltpu.VMEM)
    hbm = pl.BlockSpec(memory_space=pl.ANY)
    dma = pltpu.SemaphoreType.DMA
    weight_count = gate_weight.size + up_weight.size + down_weight.size
    return pl.pallas_call(
        functools.partial(fused_kernel, dims),
        out_shape=jax.ShapeDtypeStruct(tokens.shape, jnp.bfloat16),
        in_specs=[hbm] * 6,
        out_specs=vmem,
        scratch_shapes=[
            pltpu.VMEM(tokens.shape, jnp.bfloat16),
            pltpu.VMEM(expert_ids.shape, jnp.int32),
            pltpu.VMEM(scores.shape, jnp.float32),
            pltpu.VMEM(gate_weight.shape, jnp.bfloat16),
            pltpu.VMEM(up_weight.shape, jnp.bfloat16),
            pltpu.VMEM(down_weight.shape, jnp.bfloat16),
            pltpu.VMEM((ROWS, lanes), jnp.float32),
            pltpu.VMEM((ROWS, lanes), jnp.bfloat16),
            pltpu.VMEM((rows, lanes), jnp.bfloat16),
            pltpu.VMEM((count * TOK, width), jnp.bfloat16),
            pltpu.VMEM((experts, count * TOK, 2 * hid), jnp.float32),
            pltpu.VMEM((experts, count * TOK, 2 * hid), jnp.float32),
            pltpu.VMEM((experts, groups, count * TOK, hid), jnp.bfloat16),
            pltpu.VMEM((count * TOK, acc_w), jnp.float32),
            pltpu.VMEM((owners * ROWS, out_w), jnp.bfloat16),
            pltpu.VMEM((owners * ROWS, out_w), jnp.bfloat16),
            pltpu.VMEM((groups * ROWS, ret_lanes), jnp.bfloat16),
            pltpu.VMEM((groups * ROWS, ret_lanes), jnp.bfloat16),
            dma((3,)),
            dma((experts,)),
            dma((experts,)),
            dma((experts,)),
            dma((owners + groups - 2,)),
            dma((owners + groups - 2,)),
            dma((experts,)),
            dma((experts,)),
            dma((experts, groups - 1)),
            dma((experts, groups - 1)),
            dma((owners - 1,)),
            dma((owners - 1,)),
            dma((groups - 1,)),
            dma((groups - 1,)),
        ],
        compiler_params=pltpu.CompilerParams(
            collective_id=0, has_side_effects=True, vmem_limit_bytes=58 * 1024 * 1024
        ),
        cost_estimate=pl.CostEstimate(
            flops=2 * count * TOK * weight_count,
            bytes_accessed=2 * weight_count,
            transcendentals=count * TOK * experts * hid,
        ),
    )(tokens, expert_ids, scores, gate_weight, up_weight, down_weight)


def choose(tokens, expert_ids, scores, gate_weight, up_weight, down_weight):
    groups, owners = lax.axis_size("grp"), lax.axis_size("ex")
    experts, width, hid = gate_weight.shape
    out_w = down_weight.shape[2]
    lanes = ceil_lanes(width + 256, PACK)
    ret_lanes = ceil_lanes(out_w, PACK)
    fits = (
        tokens.shape[0] == TOK
        and lax.axis_size("side") == 2
        and groups == 4
        and owners == 4
        and hid % 128 == 0
        and out_w % 128 == 0
        and width % 128 == 0
        and width - (PACK - 1) * lanes > 0
        and experts * owners <= 128
        and experts * (2 * width * hid + groups * hid * out_w) * 2 <= 44 * 1024 * 1024
    )
    if not fits:
        return per_device(tokens, expert_ids, scores, gate_weight, up_weight, down_weight)
    dims = (groups, owners, experts, width, hid, out_w, lanes, ret_lanes)
    return fused(dims, tokens, expert_ids, scores, gate_weight, up_weight, down_weight)


def solution(mesh):
    in_specs = (
        P(("grp", "ex"), "side"),
        P(("grp", "ex"), None),
        P(("grp", "ex"), None),
        P("ex", "side", "grp"),
        P("ex", "side", "grp"),
        P("ex", None, ("side", "grp")),
    )
    out_specs = P(("grp", "ex"), "side")
    return jax.shard_map(
        choose, mesh=mesh, in_specs=in_specs, out_specs=out_specs, check_vma=False
    )
```
